512 devices in a mesh: sub: 16 (over x_lo, z), inner: 32 (over x_hi, y, core).
Axes of the slice: x: 4 (x_hi: 2, x_lo: 2; x = x_hi * 2 + x_lo), y: 8, z: 8, core: 2. Of those that a mesh axis runs over, the one named last changes fastest.
Arguments:
- front_leaf: bfloat16 [327680, 1024], P(('sub', 'inner')), may hold values from -6 to 6
- front_mid: bfloat16 [327680, 1024], P(('sub', 'inner')), may hold values from -6 to 6
- front_top: bfloat16 [327680, 1024], P(('sub', 'inner')), may hold values from -6 to 6
- dinv_leaf: bfloat16 [8192, 256], P('sub'), may hold values from -0.046875 to 0.046875
- dinv_mid: bfloat16 [4096, 256], P('sub'), may hold values from -0.046875 to 0.046875
- dinv_top: bfloat16 [2048, 256], P('sub'), may hold values from -0.046875 to 0.046875
- live_rows: int32 [3, 512], P(None, ('sub', 'inner')), may hold values from 320 to 640, as said below
- map_leaf: int32 [327680], P(('sub', 'inner')), may hold values from 0 to 1279, as said below
- map_mid: int32 [327680], P(('sub', 'inner')), may hold values from 0 to 1279, as said below
Outputs:
- contribution: bfloat16 [327680, 512], P(('sub', 'inner'))
The draws below stay inside these ranges and needn't reach their ends.
Inputs may be any that keep to these rules, and one draw needn't show every extreme that they name: `live_rows`: at each level some device block has all 640 rows live. `map_leaf`: within each block of 640 consecutive entries the codes are distinct and exactly half of them are 640 or more. `map_mid`: within each block of 640 consecutive entries the codes are distinct and exactly half of them are 640 or more.
All inputs are finite; a program needn't handle non-finite values.
Results may differ from the reference program's by a relative error of at most 0.0065.
Values may be sent and summed in bfloat16 or wider, within the bound.
A program may use at most 64 MiB of HBM per device.

```python
import jax
import jax.numpy as jnp
from jax import lax

ROWS = 640
PANEL = 512
BLOCK = 256
NEXT = 512
TOTAL = 327680
N_SUB = 16
N_INNER = 32


def draw_live_rows(key, part):
    block_total = N_SUB * N_INNER
    counts = jax.random.randint(key, (3, block_total), ROWS // 2, ROWS + 1)
    max_spots = jax.random.randint(jax.random.fold_in(key, 7), (3,), 0, block_total)
    return counts.at[jnp.arange(3), max_spots].set(ROWS).astype(jnp.int32)


def shared_codes(key):
    block_total = N_SUB * N_INNER
    block_keys = jax.random.split(key, block_total)

    def one_block(block_key):
        own_key, far_key, mix_key = jax.random.split(block_key, 3)
        own_part = jax.random.permutation(own_key, ROWS)[:ROWS // 2]
        far_part = jax.random.permutation(far_key, ROWS)[:ROWS // 2] + ROWS
        return jax.random.permutation(mix_key, jnp.concatenate([own_part, far_part]))
    return jax.vmap(one_block)(block_keys).reshape(block_total * ROWS).astype(jnp.int32)


def draw_map_leaf(key, part):
    return shared_codes(jax.random.fold_in(key, 11))


def draw_map_mid(key, part):
    return shared_codes(jax.random.fold_in(key, 13))


def block_scale(key, dims, cuts, least, largest):
    gain, own = 1.0, jax.random.fold_in(key, 6)
    for position, blocks in cuts:
        draws = jnp.exp(jax.random.uniform(jax.random.fold_in(own, position), (blocks,), jnp.float32, least / len(cuts), largest / len(cuts)))
        gain = gain * jnp.repeat(draws, dims[position] // blocks).reshape([-1 if axis == position else 1 for axis in range(len(dims))])
    return gain


def noise(stream_key, dims, deviation, reach, pieces=(), held_as=jnp.bfloat16):
    values = jax.random.normal(stream_key, dims, jnp.float32) * deviation
    if len(pieces) > 0:
        values = block_scale(stream_key, dims, pieces, -0.22, 0.18) * values
    return jnp.clip(values, min=-reach, max=reach).astype(held_as)


def setup_inputs(seed: int = 0) -> dict:
    streams_of = jax.random.split(jax.random.key(seed), 10)
    return {
        "front_leaf": noise(streams_of[0], (TOTAL, PANEL + NEXT), 1.0, 6.0, ((0, 512),)),
        "front_mid": noise(streams_of[1], (TOTAL, PANEL + NEXT), 1.0, 6.0, ((0, 512),)),
        "front_top": noise(streams_of[2], (TOTAL, PANEL + NEXT), 1.0, 6.0, ((0, 512),)),
        "dinv_leaf": noise(streams_of[3], (N_SUB * PANEL, BLOCK), (3 * BLOCK * PANEL ** 0.5) ** -0.5, 0.046875, ((0, 16),)),
        "dinv_mid": noise(streams_of[4], (N_SUB // 2 * PANEL, BLOCK), (3 * BLOCK * PANEL ** 0.5) ** -0.5, 0.046875, ((0, 16),)),
        "dinv_top": noise(streams_of[5], (N_SUB // 4 * PANEL, BLOCK), (3 * BLOCK * PANEL ** 0.5) ** -0.5, 0.046875, ((0, 16),)),
        "live_rows": draw_live_rows(jax.random.fold_in(streams_of[9], 71), 0),
        "map_leaf": draw_map_leaf(jax.random.fold_in(streams_of[9], 71), 0),
        "map_mid": draw_map_mid(jax.random.fold_in(streams_of[9], 71), 0),
    }


def level_update(front_whole, inverse, live_count, level_index):
    groups = N_SUB >> level_index
    group_rows = (N_INNER << level_index) * ROWS
    block_count = PANEL // BLOCK
    pivot_count = NEXT // (N_INNER << level_index)
    row_mask = (lax.broadcasted_iota(jnp.int32, (N_SUB * N_INNER, ROWS), 1) < live_count[:, None]).reshape(groups, group_rows)

    def one_group(items):
        front_part, inv_part, mask_part = items
        panel_part = front_part[:, :PANEL].astype(jnp.float32).reshape(group_rows, block_count, BLOCK)
        inv_table = inv_part.astype(jnp.float32).reshape(block_count, BLOCK, BLOCK)
        factor = jnp.einsum("rbk,bjk->rbj", panel_part, inv_table).reshape(group_rows, PANEL)
        factor = jnp.where(mask_part[:, None], factor, 0.0).astype(jnp.bfloat16)
        pivots = factor.reshape(group_rows // ROWS, ROWS, PANEL)[:, :pivot_count].reshape(NEXT, PANEL)
        product = jnp.dot(factor, pivots.T, preferred_element_type=jnp.float32)
        update = jnp.where(mask_part[:, None], front_part[:, PANEL:].astype(jnp.float32) - product, 0.0)
        return update.astype(jnp.bfloat16)

    result = lax.map(one_group, (front_whole.reshape(groups, group_rows, PANEL + NEXT), inverse.reshape(groups, PANEL, BLOCK), row_mask))
    return result.reshape(groups * group_rows, NEXT)


def extend_add(update, code_map, parent, level_index):
    total_rows = update.shape[0]
    row_ids = lax.iota(jnp.int32, total_rows)
    block_ids = row_ids // ROWS
    sub_ids = block_ids // N_INNER
    inner_ids = block_ids % N_INNER
    outward = code_map >= ROWS
    target_sub = jnp.where(outward, jnp.bitwise_xor(sub_ids, 1 << level_index), sub_ids)
    target_row = jnp.where(outward, code_map - ROWS, code_map)
    destination = ((target_sub * N_INNER + inner_ids) * ROWS + target_row).astype(jnp.int32)
    merged = parent[:, :NEXT].astype(jnp.float32).at[destination].add(update.astype(jnp.float32))
    return jnp.concatenate([merged.astype(jnp.bfloat16), parent[:, NEXT:]], 1)


def reference(front_leaf, front_mid, front_top, dinv_leaf, dinv_mid, dinv_top, live_rows, map_leaf, map_mid):
    update = level_update(front_leaf, dinv_leaf, live_rows[0], 0)
    parent = extend_add(update, map_leaf, front_mid, 0)
    update = level_update(parent, dinv_mid, live_rows[1], 1)
    parent = extend_add(update, map_mid, front_top, 1)
    return level_update(parent, dinv_top, live_rows[2], 2)
```

```python
import jax
import jax.numpy as jnp
from jax import lax
from jax.experimental import pallas as pl
from jax.experimental.pallas import tpu as pltpu
from jax.sharding import PartitionSpec as P

ROWS = 640
PANEL = 512
BLOCK = 256
HALF = ROWS // 2
TILE = 16
INNER = 32
F32 = jnp.float32
BF16 = jnp.bfloat16
MESH = pl.DeviceIdType.MESH

AWAY = (0, 1, -1, 2, -2, 3, -3, 4)
FAR_FIRST = (4, 3, -3, 2, -2, 1, -1)
SLOT = {d: i for i, d in enumerate(AWAY)}
BACK = {d: SLOT[-d] if -d in SLOT else SLOT[d] for d in AWAY}
CHUNKS = ((0, 176), (176, 160), (336, 160), (496, 160))
OWN_CHUNKS = ((16, 160), (176, 160))
FAR_CHUNKS = ((336, 160), (496, 160))


def mm(a, b):
    return lax.dot_general(a, b, (((1,), (0,)), ((), ())), preferred_element_type=F32)


def mmt(a, b):
    return lax.dot_general(a, b, (((1,), (1,)), ((), ())), preferred_element_type=F32)


def iota(shape, dim):
    return lax.broadcasted_iota(jnp.int32, shape, dim)


def hot(cond):
    return jnp.where(cond, 1.0, 0.0).astype(BF16)


def factor_of(panel, inv):
    return jnp.concatenate(
        [mmt(panel[:, b * BLOCK : (b + 1) * BLOCK], inv[b * BLOCK : (b + 1) * BLOCK, :]) for b in range(2)], 1
    ).astype(BF16)


def columns_of(row):
    return jnp.broadcast_to(row, (128, ROWS)).T


def body(
    leaf_hbm, mid_hbm, top_hbm, dinv0, dinv1, dinv2, live, map0, map1, out,
    head, leaf, mid, top, d1, d2, s0, s1, f0, f1, t1, fs, ms, fac, fac1, fac2,
    g, piv, perm, x0, x1, y0, y1, pm, pt, codes, local_sem, send_sem, recv_sem, g_send, g_recv,
):
    s = lax.axis_index("sub")
    j = lax.axis_index("inner")
    bit0 = lax.rem(s, 2)
    bit1 = lax.rem(lax.div(s, 2), 2)
    xh = lax.div(j, 16)
    y = lax.rem(lax.div(j, 2), 8)
    c = lax.rem(j, 2)
    near1 = s + 1 - 2 * bit0
    near2 = s + 2 - 4 * bit1
    near3 = near1 + 2 - 4 * bit1

    def inner(flip_x, dist, flip_c):
        xs = 1 - xh if flip_x else xh
        cs = 1 - c if flip_c else c
        return (s, xs * 16 + lax.rem(y + dist + 8, 8) * 2 + cs)

    def subs(flip):
        return ((s, near1, near2, near3)[flip], j)

    copies = [
        pltpu.make_async_copy(leaf_hbm.at[pl.ds(0, TILE), pl.ds(0, PANEL)], head, local_sem.at[0]),
        pltpu.make_async_copy(leaf_hbm, leaf, local_sem.at[1]),
        pltpu.make_async_copy(mid_hbm, mid, local_sem.at[2]),
        pltpu.make_async_copy(top_hbm, top, local_sem.at[3]),
    ]
    for copy in copies:
        copy.start()

    barrier = pltpu.get_barrier_semaphore()
    partners = [inner(0, d, 0) for d in FAR_FIRST] + [inner(1, d, 0) for d in AWAY] + [inner(0, 0, 1)]
    partners += [subs(f) for f in (1, 2, 3)]
    for partner in partners:
        pl.semaphore_signal(barrier, inc=1, device_id=partner, device_id_type=MESH)

    copies[0].wait()
    g[0, pl.ds(0, TILE)] = factor_of(head[...], dinv0)
    pl.semaphore_wait(barrier, len(partners))

    sends = []

    def send(src, dst, sem, target):
        copy = pltpu.make_async_remote_copy(
            src_ref=src, dst_ref=dst, send_sem=send_sem.at[len(sends)], recv_sem=recv_sem.at[sem],
            device_id=target, device_id_type=MESH,
        )
        copy.start()
        sends.append(copy)

    def arrived(ref, sem):
        pltpu.make_async_remote_copy(
            src_ref=ref, dst_ref=ref, send_sem=send_sem.at[0], recv_sem=sem, device_id=subs(1), device_id_type=MESH
        ).wait_recv()

    def g_copy(lvl, src, dst, sem, target):
        pltpu.make_async_remote_copy(
            src_ref=src, dst_ref=dst, send_sem=g_send.at[lvl], recv_sem=g_recv.at[lvl, sem],
            device_id=target, device_id_type=MESH,
        ).start()

    def gather_start(lvl):
        own = g.at[lvl, pl.ds(0, TILE)]
        for d in FAR_FIRST:
            g_copy(lvl, own, g.at[lvl, pl.ds(128 + BACK[d] * TILE, TILE)], 1, inner(1, d, 0))
            g_copy(lvl, own, g.at[lvl, pl.ds(BACK[d] * TILE, TILE)], 0, inner(0, d, 0))
        g_copy(lvl, own, g.at[lvl, pl.ds(128, TILE)], 1, inner(1, 0, 0))

    def gather_near(lvl):
        arrived(g.at[lvl, pl.ds(TILE, 112)], g_recv.at[lvl, 0])
        g_copy(lvl, g.at[lvl, pl.ds(0, 128)], g.at[lvl, pl.ds(256, 128)], 2, inner(0, 0, 1))

    def gather_far(lvl):
        arrived(g.at[lvl, pl.ds(128, 128)], g_recv.at[lvl, 1])
        g_copy(lvl, g.at[lvl, pl.ds(128, 128)], g.at[lvl, pl.ds(384, 128)], 3, inner(0, 0, 1))

    def gather_end(lvl):
        arrived(g.at[lvl, pl.ds(256, 128)], g_recv.at[lvl, 2])
        arrived(g.at[lvl, pl.ds(384, 128)], g_recv.at[lvl, 3])
        piv[...] = mm(perm[lvl], g[lvl]).astype(BF16)

    gather_start(0)
    send(dinv1, d1.at[pl.ds(pl.multiple_of(bit0 * 256, 256), 256)], 0, subs(1))
    quarter = pl.ds(pl.multiple_of((bit0 + 2 * bit1) * 128, 128), 128)
    for f in (1, 2, 3):
        send(dinv2, d2.at[quarter], f, subs(f))
    copies[2].wait()
    send(mid.at[pl.ds(0, TILE), pl.ds(0, PANEL)], pm.at[pl.ds(48, TILE)], 4, subs(1))
    copies[3].wait()
    for f in (1, 2, 3):
        send(top.at[pl.ds(0, TILE), pl.ds(0, PANEL)], pt.at[pl.ds(64 + 16 * f, TILE)], 4 + f, subs(f))

    def order(codes_row):
        down = columns_of(codes_row)[:, 0:1]
        rank = jnp.sum(jnp.where(down < codes_row, 1.0, 0.0), axis=0, keepdims=True)
        rank_down = columns_of(rank)[:, 0:1]
        at = iota((ROWS, ROWS), 1).astype(F32)
        return rank, jnp.sum(jnp.where(rank_down == at, down, 0.0), axis=0, keepdims=True)

    e0 = map0[...].astype(F32)
    e1 = map1[...].astype(F32)
    rank0, sorted0 = order(e0)
    codes[0] = jnp.broadcast_to(sorted0, (8, ROWS))
    send(codes.at[0], codes.at[1], 8, subs(1))
    rank1, sorted1 = order(e1)
    codes[2] = jnp.broadcast_to(sorted1, (8, ROWS))
    send(codes.at[2], codes.at[3], 9, subs(2))

    lanes = iota((1, ROWS), 1)
    live_f = live[...]

    def ordering(ref, codes_row, rank, early, level):
        alive = lanes < live_f[:, level : level + 1]
        slot = iota((TILE, ROWS), 0)
        wanted = jnp.where(slot < early, slot, jnp.where(slot < 2 * early, ROWS - early + slot, -1)).astype(F32)
        ref[pl.ds(0, TILE)] = hot((codes_row == wanted) & alive)
        for r, n in ((16, 160), (176, 160), (336, 160), (496, 160)):
            ref[pl.ds(r, n)] = hot((rank == (iota((n, ROWS), 0) + (r - TILE)).astype(F32)) & alive)

    ordering(s0, e0, rank0, 8, 0)
    copies[1].wait()
    for r, n in CHUNKS:
        for h in range(2):
            part = pl.ds(h * PANEL, PANEL)
            fs[pl.ds(r, n), part] = mm(s0[pl.ds(r, n)], leaf[:, part]).astype(BF16)
    gather_near(0)
    for r, n in CHUNKS:
        fac[pl.ds(r, n)] = factor_of(fs[pl.ds(r, n), pl.ds(0, PANEL)], dinv0)

    q = iota((1, PANEL), 1)
    block = (q >> 4) & 7
    dist = jnp.where(block & 1 == 1, (block + 1) >> 1, -(block >> 1))
    x_from = xh ^ ((q >> 7) & 1)
    y_from = (y + dist + 8) & 7
    j_from = x_from * 16 + y_from * 2 + (c ^ (q >> 8))
    i = q & 15
    targets = (
        j_from * 16 + i,
        (bit0 ^ (i >> 3)) * 256 + j_from * 8 + (i & 7),
        ((bit0 + 2 * bit1) ^ (i >> 2)) * 128 + j_from * 4 + (i & 3),
    )
    down = iota((PANEL, PANEL), 0)
    for lvl in range(3):
        perm[lvl] = hot(targets[lvl] == down)
    gather_far(0)

    def landing(ref, mine, far, sem, live_rows):
        arrived(codes.at[far], recv_sem.at[sem])
        at = jnp.where(lanes < HALF, codes[mine, 0:1, :], codes[far, 0:1, :] - ROWS)
        for r in range(0, ROWS, 160):
            row = iota((160, ROWS), 0) + r
            hit = row.astype(F32) == at
            if live_rows is not None:
                hit = hit & (row < live_rows)
            ref[pl.ds(r, 160)] = hot(hit)

    landing(f0, 0, 1, 8, None)
    ordering(s1, e1, rank1, 4, 1)
    for r, n in CHUNKS:
        for h in range(2):
            part = pl.ds(h * PANEL, PANEL)
            ms[pl.ds(r, n), part] = mm(s1[pl.ds(r, n)], mid[:, part]).astype(BF16)
    gather_end(0)

    def update(front, factor, rows):
        product = mmt(factor[rows], piv[...])
        return (front[rows, pl.ds(PANEL, PANEL)].astype(F32) - product).astype(BF16)

    def far_updates(front, factor, store, other, sem, flip):
        for k, (r, n) in enumerate(FAR_CHUNKS):
            store[pl.ds(k * 160, n)] = update(front, factor, pl.ds(r, n))
            send(store.at[pl.ds(k * 160, n)], other.at[pl.ds(HALF + k * 160, n)], sem + k, subs(flip))

    def own_updates(front, factor, other):
        for r, n in OWN_CHUNKS:
            other[pl.ds(r - TILE, n)] = update(front, factor, pl.ds(r, n))

    def one_of(rows, width, *columns):
        i = iota((rows, width), 0)
        k = iota((rows, width), 1)
        hit = k == columns[0](i)
        for column in columns[1:]:
            hit = hit | (k == column(i))
        return hot(hit)

    pm[pl.ds(0, TILE)] = update(fs, fac, pl.ds(0, TILE))
    send(pm.at[pl.ds(0, TILE)], pm.at[pl.ds(16, TILE)], 10, subs(1))
    far_updates(fs, fac, y0, x0, 11, 1)
    pm[pl.ds(32, TILE)] = mid[pl.ds(0, TILE), pl.ds(0, PANEL)]
    d1[pl.ds(pl.multiple_of(bit0 * 256, 256), 256)] = dinv1[...]
    arrived(d1.at[pl.ds(pl.multiple_of((1 - bit0) * 256, 256), 256)], recv_sem.at[0])
    arrived(pm.at[pl.ds(48, TILE)], recv_sem.at[4])
    arrived(pm.at[pl.ds(16, TILE)], recv_sem.at[10])
    pick1 = one_of(
        TILE, 64, lambda i: i, lambda i: jnp.where(i < 8, i + 24, i + 8), lambda i: jnp.where(i < 8, i + 32, i + 40)
    )
    g[1, pl.ds(0, TILE)] = factor_of(mm(pick1, pm[...]).astype(BF16), d1)
    gather_start(1)
    own_updates(fs, fac, x0)
    for r, n in CHUNKS:
        t1[pl.ds(r, n)] = mm(s1[pl.ds(r, n)], f0[...]).astype(BF16)
    gather_near(1)
    for k in range(2):
        arrived(x0.at[pl.ds(HALF + k * 160, 160)], recv_sem.at[11 + k])
    for r, n in CHUNKS:
        rows = pl.ds(r, n)
        whole = (ms[rows, pl.ds(0, PANEL)].astype(F32) + mm(t1[rows], x0[...])).astype(BF16)
        fac1[rows] = factor_of(whole, d1)
    gather_far(1)
    gather_end(1)

    pt[pl.ds(0, TILE)] = update(ms, fac1, pl.ds(0, TILE))
    for f in (1, 2, 3):
        send(pt.at[pl.ds(0, TILE)], pt.at[pl.ds(16 * f, TILE)], 12 + f, subs(f))
    far_updates(ms, fac1, y1, x1, 16, 2)
    pt[pl.ds(64, TILE)] = top[pl.ds(0, TILE), pl.ds(0, PANEL)]
    d2[quarter] = dinv2[...]
    for f in (1, 2, 3):
        theirs = ((0, bit0 + 2 * bit1), (1, 1 - bit0 + 2 * bit1), (2, bit0 + 2 - 2 * bit1), (3, 3 - bit0 - 2 * bit1))[f][1]
        arrived(d2.at[pl.ds(pl.multiple_of(theirs * 128, 128), 128)], recv_sem.at[f])
        arrived(pt.at[pl.ds(64 + 16 * f, TILE)], recv_sem.at[4 + f])
        arrived(pt.at[pl.ds(16 * f, TILE)], recv_sem.at[12 + f])
    pick2 = one_of(
        TILE, 128,
        lambda i: (i >> 2) * 16 + (i & 3), lambda i: ((i >> 2) ^ 2) * 16 + 4 + (i & 3), lambda i: 64 + (i >> 2) * 16 + (i & 3),
    )
    g[2, pl.ds(0, TILE)] = factor_of(mm(pick2, pt[...]).astype(BF16), d2)
    gather_start(2)
    own_updates(ms, fac1, x1)
    landing(f1, 2, 3, 9, live_f[:, 2:3])
    gather_near(2)
    for k in range(2):
        arrived(x1.at[pl.ds(HALF + k * 160, 160)], recv_sem.at[16 + k])
    for r in range(0, ROWS, 160):
        rows = pl.ds(r, 160)
        alive = (iota((160, PANEL), 0) + r) < live_f[:, 2:3]
        whole = top[rows, pl.ds(0, PANEL)].astype(F32) + mm(f1[rows], x1[...])
        fac2[rows] = factor_of(jnp.where(alive, whole, 0.0).astype(BF16), d2)
    gather_far(2)
    gather_end(2)

    for r in range(0, ROWS, 160):
        rows = pl.ds(r, 160)
        alive = (iota((160, PANEL), 0) + r) < live_f[:, 2:3]
        product = mmt(fac2[rows], piv[...])
        out[rows] = jnp.where(alive, top[rows, pl.ds(PANEL, PANEL)].astype(F32) - product, 0.0).astype(BF16)

    for copy in sends:
        copy.wait_send()
    for lvl in range(3):
        ref = g.at[lvl, pl.ds(0, 496)]
        pltpu.make_async_remote_copy(
            src_ref=ref, dst_ref=ref, send_sem=g_send.at[lvl], recv_sem=g_recv.at[lvl, 0],
            device_id=subs(1), device_id_type=MESH,
        ).wait_send()


def per_device(leaf, mid, top, dinv0, dinv1, dinv2, live_rows, map0, map1):
    vmem = pl.BlockSpec(memory_space=pltpu.VMEM)
    hbm = pl.BlockSpec(memory_space=pl.ANY)
    held = lambda *shape: pltpu.VMEM(shape, BF16)
    more = ROWS + TILE
    return pl.pallas_call(
        body,
        name="panel_steps",
        out_shape=jax.ShapeDtypeStruct((ROWS, PANEL), BF16),
        in_specs=[hbm] * 3 + [vmem] * 6,
        out_specs=vmem,
        scratch_shapes=[
            held(TILE, PANEL),
            held(ROWS, 1024),
            held(ROWS, 1024),
            held(ROWS, 1024),
            held(PANEL, BLOCK),
            held(PANEL, BLOCK),
            held(more, ROWS),
            held(more, ROWS),
            held(ROWS, ROWS),
            held(ROWS, ROWS),
            held(more, ROWS),
            held(more, 1024),
            held(more, 1024),
            held(more, PANEL),
            held(more, PANEL),
            held(ROWS, PANEL),
            held(3, PANEL, PANEL),
            held(PANEL, PANEL),
            held(3, PANEL, PANEL),
            held(ROWS, PANEL),
            held(ROWS, PANEL),
            held(HALF, PANEL),
            held(HALF, PANEL),
            held(64, PANEL),
            held(128, PANEL),
            pltpu.VMEM((4, 8, ROWS), F32),
            pltpu.SemaphoreType.DMA((4,)),
            pltpu.SemaphoreType.DMA((24,)),
            pltpu.SemaphoreType.DMA((18,)),
            pltpu.SemaphoreType.DMA((3,)),
            pltpu.SemaphoreType.DMA((3, 4)),
        ],
        compiler_params=pltpu.CompilerParams(
            collective_id=0, has_side_effects=True, vmem_limit_bytes=48 * 2**20
        ),
    )(leaf, mid, top, dinv0, dinv1, dinv2, live_rows.reshape(1, 3), map0.reshape(1, ROWS), map1.reshape(1, ROWS))


def solution(mesh):
    rows = P(("sub", "inner"), None)
    placed = (
        rows, rows, rows, P("sub", None), P("sub", None), P("sub", None),
        P(None, ("sub", "inner")), P(("sub", "inner")), P(("sub", "inner")),
    )
    return jax.shard_map(per_device, mesh=mesh, in_specs=placed, out_specs=rows, check_vma=False)
```

```python
import jax
import jax.numpy as jnp
from jax import lax
from jax.experimental import pallas as pl
from jax.experimental.pallas import tpu as pltpu
from jax.sharding import PartitionSpec as P

ROWS = 640
PANEL = 512
BLOCK = 256
HALF = ROWS // 2
TILE = 16
INNER = 32
F32 = jnp.float32
BF16 = jnp.bfloat16
MESH = pl.DeviceIdType.MESH

AWAY = (0, 1, -1, 2, -2, 3, -3, 4)
FAR_FIRST = (4, 3, -3, 2, -2, 1, -1)
SLOT = {d: i for i, d in enumerate(AWAY)}
BACK = {d: SLOT[-d] if -d in SLOT else SLOT[d] for d in AWAY}
CHUNKS = ((0, 336), (336, 320))
OWN_CHUNKS = ((16, 320),)
FAR_CHUNKS = ((336, 192), (528, 128))


def mm(a, b):
    return lax.dot_general(a, b, (((1,), (0,)), ((), ())), preferred_element_type=F32)


def mmt(a, b):
    return lax.dot_general(a, b, (((1,), (1,)), ((), ())), preferred_element_type=F32)


def iota(shape, dim):
    return lax.broadcasted_iota(jnp.int32, shape, dim)


def hot(cond):
    return jnp.where(cond, 1.0, 0.0).astype(BF16)


def factor_of(panel, inv):
    return jnp.concatenate(
        [mmt(panel[:, b * BLOCK : (b + 1) * BLOCK], inv[b * BLOCK : (b + 1) * BLOCK, :]) for b in range(2)], 1
    ).astype(BF16)


def columns_of(row):
    return jnp.broadcast_to(row, (128, ROWS)).T


def body(
    leaf_hbm, mid_hbm, top_hbm, dinv0_hbm, dinv1_hbm, dinv2_hbm, live_hbm, map0_hbm, map1_hbm, out,
    lead, leaf, mid, top, dinv0, live, map0, map1, d1, d2, s0, s1, f0, f1, t1, fs, ms, fac, fac1, fac2,
    g, piv, perm, x0, x1, y0, y1, pm, pt, pick1, pick2, acc, res, codes, local_sem, send_sem, recv_sem, g_send, g_recv,
):
    s = lax.axis_index("sub")
    j = lax.axis_index("inner")
    bit0 = lax.rem(s, 2)
    bit1 = lax.rem(lax.div(s, 2), 2)
    xh = lax.div(j, 16)
    y = lax.rem(lax.div(j, 2), 8)
    c = lax.rem(j, 2)
    near1 = s + 1 - 2 * bit0
    near2 = s + 2 - 4 * bit1
    near3 = near1 + 2 - 4 * bit1

    def inner(flip_x, dist, flip_c):
        xs = 1 - xh if flip_x else xh
        cs = 1 - c if flip_c else c
        return (s, xs * 16 + lax.rem(y + dist + 8, 8) * 2 + cs)

    def subs(flip):
        return ((s, near1, near2, near3)[flip], j)

    copies = [
        pltpu.make_async_copy(leaf_hbm.at[pl.ds(0, TILE), pl.ds(0, PANEL)], lead.at[xh, y, c], local_sem.at[0]),
        pltpu.make_async_copy(dinv0_hbm, dinv0, local_sem.at[1]),
        pltpu.make_async_copy(map0_hbm, map0, local_sem.at[2]),
        pltpu.make_async_copy(map1_hbm, map1, local_sem.at[3]),
        pltpu.make_async_copy(live_hbm, live, local_sem.at[4]),
        pltpu.make_async_copy(leaf_hbm, leaf, local_sem.at[5]),
        pltpu.make_async_copy(mid_hbm, mid, local_sem.at[6]),
        pltpu.make_async_copy(top_hbm, top, local_sem.at[7]),
        pltpu.make_async_copy(dinv1_hbm, d1.at[pl.ds(pl.multiple_of(bit0 * 256, 256), 256)], local_sem.at[8]),
        pltpu.make_async_copy(
            dinv2_hbm, d2.at[pl.ds(pl.multiple_of((bit0 + 2 * bit1) * 128, 128), 128)], local_sem.at[9]
        ),
    ]
    barrier = pltpu.get_barrier_semaphore()
    partners = [inner(0, d, 0) for d in FAR_FIRST] + [inner(1, d, 0) for d in AWAY[:5]] + [inner(1, 0, 1), inner(0, 0, 1)]
    partners += [subs(f) for f in (1, 2, 3)]
    for partner in partners:
        pl.semaphore_signal(barrier, inc=1, device_id=partner, device_id_type=MESH)

    for copy in copies:
        copy.start()
    pl.semaphore_wait(barrier, len(partners))

    sends = []

    def send(src, dst, sem, target):
        copy = pltpu.make_async_remote_copy(
            src_ref=src, dst_ref=dst, send_sem=send_sem.at[len(sends)], recv_sem=recv_sem.at[sem],
            device_id=target, device_id_type=MESH,
        )
        copy.start()
        sends.append(copy)

    def arrived(ref, sem):
        pltpu.make_async_remote_copy(
            src_ref=ref, dst_ref=ref, send_sem=send_sem.at[0], recv_sem=sem, device_id=subs(1), device_id_type=MESH
        ).wait_recv()

    def g_copy(lvl, src, dst, sem, target):
        pltpu.make_async_remote_copy(
            src_ref=src, dst_ref=dst, send_sem=g_send.at[lvl], recv_sem=g_recv.at[lvl, sem],
            device_id=target, device_id_type=MESH,
        ).start()

    def place(lvl, flip_x, d, mine):
        if lvl == 0:
            return lead.at[xh, y, c] if mine else lead.at[1 - xh if flip_x else xh, lax.rem(y + d + 8, 8), c]
        return g.at[lvl - 1, pl.ds(128 * flip_x + (BACK[d] if mine else SLOT[d]) * TILE, TILE)]

    def column(lvl, flip_x, flip_c):
        if lvl == 0:
            return lead.at[1 - xh if flip_x else xh, :, 1 - c if flip_c else c]
        return g.at[lvl - 1, pl.ds(256 * flip_c + 128 * flip_x, 128)]

    def seven(lvl):
        return lead.at[0, pl.ds(0, 7), 0] if lvl == 0 else g.at[lvl - 1, pl.ds(0, 112)]

    def gather_start(lvl, own):
        for d in FAR_FIRST:
            g_copy(lvl, own, place(lvl, 0, d, True), 0, inner(0, d, 0))
        for d in FAR_FIRST[3:] + (0,):
            g_copy(lvl, own, place(lvl, 1, d, True), 1, inner(1, d, 0))

    def y_landed(lvl):
        arrived(seven(lvl), g_recv.at[lvl, 0])
        for d in FAR_FIRST[:3]:
            part = place(lvl, 0, d, False)
            for flip_c in (0, 1):
                to = part if lvl == 0 else g.at[lvl - 1, pl.ds(256 * flip_c + 128 + SLOT[d] * TILE, TILE)]
                g_copy(lvl, part, to, 4 + flip_c, inner(1, 0, flip_c))
        part = column(lvl, 0, 0)
        g_copy(lvl, part, part if lvl == 0 else column(lvl, 0, 1), 2, inner(0, 0, 1))

    def five(lvl):
        return lead.at[0, pl.ds(0, 5), 0] if lvl == 0 else g.at[lvl - 1, pl.ds(128, 80)]

    def three(lvl, flip_c):
        return lead.at[0, pl.ds(0, 3), 0] if lvl == 0 else g.at[lvl - 1, pl.ds(256 * flip_c + 208, 48)]

    def x_landed(lvl):
        arrived(five(lvl), g_recv.at[lvl, 1])
        if lvl == 0:
            for d in (0,) + FAR_FIRST[3:]:
                part = place(0, 1, d, False)
                g_copy(lvl, part, part, 3, inner(0, 0, 1))
        else:
            g_copy(lvl, five(lvl), g.at[lvl - 1, pl.ds(384, 80)], 3, inner(0, 0, 1))

    def gather_end(lvl):
        arrived(three(lvl, 0), g_recv.at[lvl, 4])
        if lvl > 0:
            half = mm(perm[lvl - 1, :, pl.ds(0, 256)], g[lvl - 1, pl.ds(0, 256)])
        arrived(column(lvl, 0, 1), g_recv.at[lvl, 2])
        arrived(five(lvl) if lvl == 0 else g.at[lvl - 1, pl.ds(384, 80)], g_recv.at[lvl, 3])
        arrived(three(lvl, 1), g_recv.at[lvl, 5])
        if lvl > 0:
            half += mm(perm[lvl - 1, :, pl.ds(256, 256)], g[lvl - 1, pl.ds(256, 256)])
            piv[...] = half.astype(BF16)
        else:
            piv[...] = factor_of(lead[...].reshape(PANEL, PANEL), dinv0)

    gather_start(0, leaf_hbm.at[pl.ds(0, TILE), pl.ds(0, PANEL)])
    quarter = pl.ds(pl.multiple_of((bit0 + 2 * bit1) * 128 + c * 64, 64), 64)
    half = pl.ds(pl.multiple_of(bit0 * 256 + c * 128, 128), 128)
    send(dinv1_hbm.at[pl.ds(pl.multiple_of(c * 128, 128), 128)], d1.at[half], 0, subs(1))
    send(mid_hbm.at[pl.ds(0, TILE), pl.ds(0, PANEL)], pm.at[pl.ds(48, TILE)], 4, subs(1))
    for f in (1, 2, 3):
        send(top_hbm.at[pl.ds(0, TILE), pl.ds(0, PANEL)], pt.at[pl.ds(64 + 16 * f, TILE)], 4 + f, subs(f))
        send(dinv2_hbm.at[pl.ds(pl.multiple_of(c * 64, 64), 64)], d2.at[quarter], f, subs(f))

    def order(codes_row):
        down = columns_of(codes_row)[:, 0:1]
        rank = jnp.sum(jnp.where(down < codes_row, 1.0, 0.0), axis=0, keepdims=True)
        rank_down = columns_of(rank)[:, 0:1]
        at = iota((ROWS, ROWS), 1).astype(F32)
        return rank, jnp.sum(jnp.where(rank_down == at, down, 0.0), axis=0, keepdims=True)

    for copy in copies[2:5]:
        copy.wait()
    e0 = map0[...].astype(F32).reshape(1, ROWS)
    e1 = map1[...].astype(F32).reshape(1, ROWS)
    rank0, sorted0 = order(e0)
    codes[0] = jnp.broadcast_to(sorted0, (8, ROWS))
    send(codes.at[0], codes.at[1], 8, subs(1))
    rank1, sorted1 = order(e1)
    codes[2] = jnp.broadcast_to(sorted1, (8, ROWS))
    send(codes.at[2], codes.at[3], 9, subs(2))

    lanes = iota((1, ROWS), 1)
    live_f = live[...]

    def ordering(ref, codes_row, rank, early, level):
        alive = lanes < live_f[:, level : level + 1]
        slot = iota((TILE, ROWS), 0)
        wanted = jnp.where(slot < early, slot, jnp.where(slot < 2 * early, ROWS - early + slot, -1)).astype(F32)
        ref[pl.ds(0, TILE)] = hot((codes_row == wanted) & alive)
        for r, n in ((16, 160), (176, 160), (336, 160), (496, 160)):
            ref[pl.ds(r, n)] = hot((rank == (iota((n, ROWS), 0) + (r - TILE)).astype(F32)) & alive)

    ordering(s0, e0, rank0, 8, 0)
    copies[5].wait()

    def ordered(ref, order_ref, front, chunks):
        for r, n in chunks:
            for h in range(2):
                part = pl.ds(h * PANEL, PANEL)
                ref[pl.ds(r, n), part] = mm(order_ref[pl.ds(r, n)], front[:, part]).astype(BF16)

    ordered(fs, s0, leaf, CHUNKS)
    copies[1].wait()
    for r, n in CHUNKS:
        fac[pl.ds(r, n)] = factor_of(fs[pl.ds(r, n), pl.ds(0, PANEL)], dinv0)
    copies[0].wait()
    y_landed(0)
    got = d1.at[pl.ds(pl.multiple_of((1 - bit0) * 256 + c * 128, 128), 128)]
    arrived(got, recv_sem.at[0])
    send(got, got, 18, inner(0, 0, 1))

    q = iota((1, PANEL), 1)
    block = (q >> 4) & 7
    dist = jnp.where(block & 1 == 1, (block + 1) >> 1, -(block >> 1))
    x_from = xh ^ ((q >> 7) & 1)
    y_from = (y + dist + 8) & 7
    j_from = x_from * 16 + y_from * 2 + (c ^ (q >> 8))
    i = q & 15
    targets = (
        (bit0 ^ (i >> 3)) * 256 + j_from * 8 + (i & 7),
        ((bit0 + 2 * bit1) ^ (i >> 2)) * 128 + j_from * 4 + (i & 3),
    )
    down = iota((PANEL, PANEL), 0)
    for lvl in range(2):
        perm[lvl] = hot(targets[lvl] == down)

    def one_of(ref, *columns):
        i = iota(ref.shape, 0)
        k = iota(ref.shape, 1)
        hit = k == columns[0](i)
        for column in columns[1:]:
            hit = hit | (k == column(i))
        ref[...] = hot(hit)

    one_of(
        pick1, lambda i: i, lambda i: jnp.where(i < 8, i + 24, i + 8), lambda i: jnp.where(i < 8, i + 32, i + 40)
    )
    one_of(
        pick2,
        lambda i: (i >> 2) * 16 + (i & 3), lambda i: ((i >> 2) ^ 2) * 16 + 4 + (i & 3), lambda i: 64 + (i >> 2) * 16 + (i & 3),
    )
    copies[6].wait()
    pm[pl.ds(32, TILE)] = mid[pl.ds(0, TILE), pl.ds(0, PANEL)]
    ordering(s1, e1, rank1, 4, 1)
    x_landed(0)
    gather_end(0)

    def landing(ref, mine, far, sem, live_rows):
        arrived(codes.at[far], recv_sem.at[sem])
        at = jnp.where(lanes < HALF, codes[mine, 0:1, :], codes[far, 0:1, :] - ROWS)
        for r in range(0, ROWS, 160):
            row = iota((160, ROWS), 0) + r
            hit = row.astype(F32) == at
            if live_rows is not None:
                hit = hit & (row < live_rows)
            ref[pl.ds(r, 160)] = hot(hit)

    def update(front, factor, rows):
        product = mmt(factor[rows], piv[...])
        return (front[rows, pl.ds(PANEL, PANEL)].astype(F32) - product).astype(BF16)

    def far_updates(front, factor, store, other, sem, flip):
        later = []
        for k, (r, n) in enumerate(FAR_CHUNKS):
            at = r - FAR_CHUNKS[0][0]
            store[pl.ds(at, n)] = update(front, factor, pl.ds(r, n))
            later.append((store.at[pl.ds(at, n)], other.at[pl.ds(HALF + at, n)], sem + k, subs(flip)))
        return later

    def own_updates(front, factor, other):
        for r, n in OWN_CHUNKS:
            other[pl.ds(r - TILE, n)] = update(front, factor, pl.ds(r, n))

    def first_part(front, place, other, chunks):
        for r, n in chunks:
            rows = pl.ds(r, n)
            acc[rows] = front[rows, pl.ds(0, PANEL)].astype(F32) + mm(place[rows, pl.ds(0, 256)], other[pl.ds(0, 256)])

    def second_part(place, other, sem, chunks):
        arrived(other.at[pl.ds(HALF, 192)], recv_sem.at[sem])
        for r, n in chunks:
            rows = pl.ds(r, n)
            acc[rows] += mm(place[rows, pl.ds(256, 256)], other[pl.ds(256, 256)])

    def last_part(place, other, sem, chunks, inv, factor, live_rows):
        arrived(other.at[pl.ds(512, 128)], recv_sem.at[sem])
        for r, n in chunks:
            rows = pl.ds(r, n)
            whole = acc[rows] + mm(place[rows, pl.ds(512, 128)], other[pl.ds(512, 128)])
            if live_rows is not None:
                whole = jnp.where((iota((n, PANEL), 0) + r) < live_rows, whole, 0.0)
            factor[rows] = factor_of(whole.astype(BF16), inv)

    pm[pl.ds(0, TILE)] = update(fs, fac, pl.ds(0, TILE))
    send(pm.at[pl.ds(0, TILE)], pm.at[pl.ds(16, TILE)], 10, subs(1))
    later = far_updates(fs, fac, y0, x0, 11, 1)
    copies[8].wait()
    arrived(d1.at[pl.ds(pl.multiple_of((1 - bit0) * 256 + (1 - c) * 128, 128), 128)], recv_sem.at[18])
    arrived(pm.at[pl.ds(48, TILE)], recv_sem.at[4])
    arrived(pm.at[pl.ds(16, TILE)], recv_sem.at[10])
    g[0, pl.ds(0, TILE)] = factor_of(mm(pick1[...], pm[...]).astype(BF16), d1)
    gather_start(1, g.at[0, pl.ds(0, TILE)])
    for part in later:
        send(*part)
    own_updates(fs, fac, x0)
    quarters = (0, 1 - bit0 + 2 * bit1, bit0 + 2 - 2 * bit1, 3 - bit0 - 2 * bit1)
    for f in (1, 2, 3):
        got = d2.at[pl.ds(pl.multiple_of(quarters[f] * 128 + c * 64, 64), 64)]
        arrived(got, recv_sem.at[f])
        send(got, got, 18 + f, inner(0, 0, 1))
    landing(f0, 0, 1, 8, None)
    for r, n in CHUNKS:
        t1[pl.ds(r, n)] = mm(s1[pl.ds(r, n)], f0[...]).astype(BF16)
    ordered(ms, s1, mid, CHUNKS)
    first_part(ms, t1, x0, CHUNKS)
    y_landed(1)
    copies[7].wait()
    pt[pl.ds(64, TILE)] = top[pl.ds(0, TILE), pl.ds(0, PANEL)]
    second_part(t1, x0, 11, CHUNKS)
    x_landed(1)
    last_part(t1, x0, 12, CHUNKS, d1, fac1, None)
    gather_end(1)

    pt[pl.ds(0, TILE)] = update(ms, fac1, pl.ds(0, TILE))
    for f in (2, 1, 3):
        send(pt.at[pl.ds(0, TILE)], pt.at[pl.ds(16 * f, TILE)], 12 + f, subs(f))
    later = far_updates(ms, fac1, y1, x1, 16, 2)
    copies[9].wait()
    for f in (1, 2, 3):
        arrived(d2.at[pl.ds(pl.multiple_of(quarters[f] * 128 + (1 - c) * 64, 64), 64)], recv_sem.at[18 + f])
        arrived(pt.at[pl.ds(64 + 16 * f, TILE)], recv_sem.at[4 + f])
        arrived(pt.at[pl.ds(16 * f, TILE)], recv_sem.at[12 + f])
    g[1, pl.ds(0, TILE)] = factor_of(mm(pick2[...], pt[...]).astype(BF16), d2)
    gather_start(2, g.at[1, pl.ds(0, TILE)])
    for part in later:
        send(*part)
    even = ((0, 320), (320, 320))
    own_updates(ms, fac1, x1)
    landing(f1, 2, 3, 9, live_f[:, 2:3])
    first_part(top, f1, x1, even)
    y_landed(2)
    x_landed(2)
    second_part(f1, x1, 16, even)
    gather_end(2)
    last_part(f1, x1, 17, even, d2, fac2, live_f[:, 2:3])

    results = []
    for r, n in even:
        rows = pl.ds(r, n)
        alive = (iota((n, PANEL), 0) + r) < live_f[:, 2:3]
        product = mmt(fac2[rows], piv[...])
        res[rows] = jnp.where(alive, top[rows, pl.ds(PANEL, PANEL)].astype(F32) - product, 0.0).astype(BF16)
        results.append(pltpu.make_async_copy(res.at[rows], out.at[rows], local_sem.at[len(results)]))
        results[-1].start()
    for copy in sends:
        copy.wait_send()
    for lvl in range(3):
        ref = fs.at[pl.ds(0, 496), pl.ds(0, PANEL)]
        pltpu.make_async_remote_copy(
            src_ref=ref, dst_ref=ref, send_sem=g_send.at[lvl], recv_sem=g_recv.at[lvl, 0],
            device_id=subs(1), device_id_type=MESH,
        ).wait_send()
    for copy in results:
        copy.wait()


def per_device(leaf, mid, top, dinv0, dinv1, dinv2, live_rows, map0, map1):
    hbm = pl.BlockSpec(memory_space=pl.ANY)
    held = lambda *shape: pltpu.VMEM(shape, BF16)
    more = ROWS + TILE
    return pl.pallas_call(
        body,
        name="panel_steps",
        out_shape=jax.ShapeDtypeStruct((ROWS, PANEL), BF16),
        in_specs=[hbm] * 9,
        out_specs=hbm,
        scratch_shapes=[
            held(2, 8, 2, TILE, PANEL),
            held(ROWS, 1024),
            held(ROWS, 1024),
            held(ROWS, 1024),
            held(PANEL, BLOCK),
            pltpu.VMEM((1, 3), jnp.int32),
            pltpu.VMEM((ROWS,), jnp.int32),
            pltpu.VMEM((ROWS,), jnp.int32),
            held(PANEL, BLOCK),
            held(PANEL, BLOCK),
            held(more, ROWS),
            held(more, ROWS),
            held(ROWS, ROWS),
            held(ROWS, ROWS),
            held(more, ROWS),
            held(more, 1024),
            held(more, 1024),
            held(more, PANEL),
            held(more, PANEL),
            held(ROWS, PANEL),
            held(2, PANEL, PANEL),
            held(PANEL, PANEL),
            held(2, PANEL, PANEL),
            held(ROWS, PANEL),
            held(ROWS, PANEL),
            held(HALF, PANEL),
            held(HALF, PANEL),
            held(64, PANEL),
            held(128, PANEL),
            held(TILE, 64),
            held(TILE, 128),
            pltpu.VMEM((more, PANEL), F32),
            held(ROWS, PANEL),
            pltpu.VMEM((4, 8, ROWS), F32),
            pltpu.SemaphoreType.DMA((10,)),
            pltpu.SemaphoreType.DMA((24,)),
            pltpu.SemaphoreType.DMA((22,)),
            pltpu.SemaphoreType.DMA((3,)),
            pltpu.SemaphoreType.DMA((3, 6)),
        ],
        compiler_params=pltpu.CompilerParams(
            collective_id=0, has_side_effects=True, vmem_limit_bytes=60 * 2**20
        ),
    )(leaf, mid, top, dinv0, dinv1, dinv2, live_rows.reshape(1, 3), map0, map1)


def solution(mesh):
    rows = P(("sub", "inner"), None)
    placed = (
        rows, rows, rows, P("sub", None), P("sub", None), P("sub", None),
        P(None, ("sub", "inner")), P(("sub", "inner")), P(("sub", "inner")),
    )
    return jax.shard_map(per_device, mesh=mesh, in_specs=placed, out_specs=rows, check_vma=False)
```

```python
import jax
import jax.numpy as jnp
from jax import lax
from jax.experimental import pallas as pl
from jax.experimental.pallas import tpu as pltpu
from jax.sharding import PartitionSpec as P

ROWS = 640
PANEL = 512
BLOCK = 256
HALF = ROWS // 2
TILE = 16
INNER = 32
F32 = jnp.float32
BF16 = jnp.bfloat16
MESH = pl.DeviceIdType.MESH

AWAY = (0, 1, -1, 2, -2, 3, -3, 4)
FAR_FIRST = (4, 3, -3, 2, -2, 1, -1)
SLOT = {d: i for i, d in enumerate(AWAY)}
BACK = {d: SLOT[-d] if -d in SLOT else SLOT[d] for d in AWAY}
CHUNKS = ((0, 336), (336, 320))
OWN_CHUNKS = ((16, 320),)
FAR_CHUNKS = ((336, 192), (528, 128))


def mm(a, b):
    return lax.dot_general(a, b, (((1,), (0,)), ((), ())), preferred_element_type=F32)


def mmt(a, b):
    return lax.dot_general(a, b, (((1,), (1,)), ((), ())), preferred_element_type=F32)


def iota(shape, dim):
    return lax.broadcasted_iota(jnp.int32, shape, dim)


def hot(cond):
    return jnp.where(cond, 1.0, 0.0).astype(BF16)


def factor_of(panel, inv):
    return jnp.concatenate(
        [mmt(panel[:, b * BLOCK : (b + 1) * BLOCK], inv[b * BLOCK : (b + 1) * BLOCK, :]) for b in range(2)], 1
    ).astype(BF16)


def columns_of(row):
    return jnp.broadcast_to(row, (128, ROWS)).T


def body(
    leaf_hbm, mid_hbm, top_hbm, dinv0_hbm, dinv1_hbm, dinv2_hbm, live_hbm, map0_hbm, map1_hbm, out,
    lead, leaf, mid, top, dinv0, live, map0, map1, d1, d2, s0, s1, f0, f1, t1, fs, ms, fac, fac1, fac2,
    g, piv, perm, x0, x1, y0, y1, pm, pt, pick1, pick2, acc, res, codes, local_sem, send_sem, recv_sem, g_send, g_recv,
):
    s = lax.axis_index("sub")
    j = lax.axis_index("inner")
    bit0 = lax.rem(s, 2)
    bit1 = lax.rem(lax.div(s, 2), 2)
    xh = lax.div(j, 16)
    y = lax.rem(lax.div(j, 2), 8)
    c = lax.rem(j, 2)
    near1 = s + 1 - 2 * bit0
    near2 = s + 2 - 4 * bit1
    near3 = near1 + 2 - 4 * bit1

    def inner(flip_x, dist, flip_c):
        xs = 1 - xh if flip_x else xh
        cs = 1 - c if flip_c else c
        return (s, xs * 16 + lax.rem(y + dist + 8, 8) * 2 + cs)

    def subs(flip):
        return ((s, near1, near2, near3)[flip], j)

    copies = [
        pltpu.make_async_copy(leaf_hbm.at[pl.ds(0, TILE), pl.ds(0, PANEL)], lead.at[xh, y, c], local_sem.at[0]),
        pltpu.make_async_copy(dinv0_hbm, dinv0, local_sem.at[1]),
        pltpu.make_async_copy(map0_hbm, map0, local_sem.at[2]),
        pltpu.make_async_copy(map1_hbm, map1, local_sem.at[3]),
        pltpu.make_async_copy(live_hbm, live, local_sem.at[4]),
        pltpu.make_async_copy(leaf_hbm, leaf, local_sem.at[5]),
        pltpu.make_async_copy(mid_hbm, mid, local_sem.at[6]),
        pltpu.make_async_copy(top_hbm, top, local_sem.at[7]),
        pltpu.make_async_copy(dinv1_hbm, d1.at[pl.ds(pl.multiple_of(bit0 * 256, 256), 256)], local_sem.at[8]),
        pltpu.make_async_copy(
            dinv2_hbm, d2.at[pl.ds(pl.multiple_of((bit0 + 2 * bit1) * 128, 128), 128)], local_sem.at[9]
        ),
    ]
    barrier = pltpu.get_barrier_semaphore()
    partners = [inner(0, d, 0) for d in FAR_FIRST] + [inner(1, d, 0) for d in AWAY[:5]] + [inner(1, 0, 1), inner(0, 0, 1)]
    partners += [subs(f) for f in (1, 2, 3)]
    for partner in partners:
        pl.semaphore_signal(barrier, inc=1, device_id=partner, device_id_type=MESH)

    for copy in copies:
        copy.start()
    pl.semaphore_wait(barrier, len(partners))

    sends = []

    def send(src, dst, sem, target):
        copy = pltpu.make_async_remote_copy(
            src_ref=src, dst_ref=dst, send_sem=send_sem.at[len(sends)], recv_sem=recv_sem.at[sem],
            device_id=target, device_id_type=MESH,
        )
        copy.start()
        sends.append(copy)

    def arrived(ref, sem):
        pltpu.make_async_remote_copy(
            src_ref=ref, dst_ref=ref, send_sem=send_sem.at[0], recv_sem=sem, device_id=subs(1), device_id_type=MESH
        ).wait_recv()

    def g_copy(lvl, src, dst, sem, target):
        pltpu.make_async_remote_copy(
            src_ref=src, dst_ref=dst, send_sem=g_send.at[lvl], recv_sem=g_recv.at[lvl, sem],
            device_id=target, device_id_type=MESH,
        ).start()

    def place(lvl, flip_x, d, mine):
        if lvl == 0:
            return lead.at[xh, y, c] if mine else lead.at[1 - xh if flip_x else xh, lax.rem(y + d + 8, 8), c]
        return g.at[lvl - 1, pl.ds(128 * flip_x + (BACK[d] if mine else SLOT[d]) * TILE, TILE)]

    def column(lvl, flip_x, flip_c):
        if lvl == 0:
            return lead.at[1 - xh if flip_x else xh, :, 1 - c if flip_c else c]
        return g.at[lvl - 1, pl.ds(256 * flip_c + 128 * flip_x, 128)]

    def four(lvl):
        return lead.at[0, pl.ds(0, 4), 0] if lvl == 0 else g.at[lvl - 1, pl.ds(16, 64)]

    def gather_start(lvl, own):
        for d in FAR_FIRST:
            g_copy(lvl, own, place(lvl, 0, d, True), 6 if abs(d) > 2 else 0, inner(0, d, 0))
        for d in FAR_FIRST[3:] + (0,):
            g_copy(lvl, own, place(lvl, 1, d, True), 1, inner(1, d, 0))

    def y_landed(lvl):
        arrived(three(lvl, 0), g_recv.at[lvl, 6])
        for d in FAR_FIRST[:3]:
            part = place(lvl, 0, d, False)
            for flip_c in (0, 1):
                to = part if lvl == 0 else g.at[lvl - 1, pl.ds(256 * flip_c + 128 + SLOT[d] * TILE, TILE)]
                g_copy(lvl, part, to, 4 + flip_c, inner(1, 0, flip_c))
        arrived(four(lvl), g_recv.at[lvl, 0])
        part = column(lvl, 0, 0)
        g_copy(lvl, part, part if lvl == 0 else column(lvl, 0, 1), 2, inner(0, 0, 1))

    def five(lvl):
        return lead.at[0, pl.ds(0, 5), 0] if lvl == 0 else g.at[lvl - 1, pl.ds(128, 80)]

    def three(lvl, flip_c):
        return lead.at[0, pl.ds(0, 3), 0] if lvl == 0 else g.at[lvl - 1, pl.ds(256 * flip_c + 208, 48)]

    def x_landed(lvl):
        arrived(five(lvl), g_recv.at[lvl, 1])
        if lvl == 0:
            for d in (0,) + FAR_FIRST[3:]:
                part = place(0, 1, d, False)
                g_copy(lvl, part, part, 3, inner(0, 0, 1))
        else:
            g_copy(lvl, five(lvl), g.at[lvl - 1, pl.ds(384, 80)], 3, inner(0, 0, 1))

    def gather_end(lvl):
        arrived(three(lvl, 0), g_recv.at[lvl, 4])
        if lvl > 0:
            half = mm(perm[lvl - 1, :, pl.ds(0, 256)], g[lvl - 1, pl.ds(0, 256)])
        arrived(column(lvl, 0, 1), g_recv.at[lvl, 2])
        arrived(five(lvl) if lvl == 0 else g.at[lvl - 1, pl.ds(384, 80)], g_recv.at[lvl, 3])
        arrived(three(lvl, 1), g_recv.at[lvl, 5])
        if lvl > 0:
            half += mm(perm[lvl - 1, :, pl.ds(256, 256)], g[lvl - 1, pl.ds(256, 256)])
            piv[...] = half.astype(BF16)
        else:
            piv[...] = factor_of(lead[...].reshape(PANEL, PANEL), dinv0)

    gather_start(0, leaf_hbm.at[pl.ds(0, TILE), pl.ds(0, PANEL)])
    quarter = pl.ds(pl.multiple_of((bit0 + 2 * bit1) * 128 + c * 64, 64), 64)
    half = pl.ds(pl.multiple_of(bit0 * 256 + c * 128, 128), 128)
    send(dinv1_hbm.at[pl.ds(pl.multiple_of(c * 128, 128), 128)], d1.at[half], 0, subs(1))
    send(mid_hbm.at[pl.ds(0, TILE), pl.ds(0, PANEL)], pm.at[pl.ds(48, TILE)], 4, subs(1))
    for f in (1, 2, 3):
        send(top_hbm.at[pl.ds(0, TILE), pl.ds(0, PANEL)], pt.at[pl.ds(64 + 16 * f, TILE)], 4 + f, subs(f))
        send(dinv2_hbm.at[pl.ds(pl.multiple_of(c * 64, 64), 64)], d2.at[quarter], f, subs(f))

    def order(codes_row):
        down = columns_of(codes_row)[:, 0:1]
        rank = jnp.sum(jnp.where(down < codes_row, 1.0, 0.0), axis=0, keepdims=True)
        rank_down = columns_of(rank)[:, 0:1]
        at = iota((ROWS, ROWS), 1).astype(F32)
        return rank, jnp.sum(jnp.where(rank_down == at, down, 0.0), axis=0, keepdims=True)

    for copy in copies[2:5]:
        copy.wait()
    e0 = map0[...].astype(F32).reshape(1, ROWS)
    e1 = map1[...].astype(F32).reshape(1, ROWS)
    rank0, sorted0 = order(e0)
    codes[0] = jnp.broadcast_to(sorted0, (8, ROWS))
    send(codes.at[0], codes.at[1], 8, subs(1))
    rank1, sorted1 = order(e1)
    codes[2] = jnp.broadcast_to(sorted1, (8, ROWS))
    send(codes.at[2], codes.at[3], 9, subs(2))

    lanes = iota((1, ROWS), 1)
    live_f = live[...]

    def ordering(ref, codes_row, rank, early, level):
        alive = lanes < live_f[:, level : level + 1]
        slot = iota((TILE, ROWS), 0)
        wanted = jnp.where(slot < early, slot, jnp.where(slot < 2 * early, ROWS - early + slot, -1)).astype(F32)
        ref[pl.ds(0, TILE)] = hot((codes_row == wanted) & alive)
        for r, n in ((16, 160), (176, 160), (336, 160), (496, 160)):
            ref[pl.ds(r, n)] = hot((rank == (iota((n, ROWS), 0) + (r - TILE)).astype(F32)) & alive)

    ordering(s0, e0, rank0, 8, 0)
    copies[5].wait()

    def ordered(ref, order_ref, front, chunks):
        for r, n in chunks:
            for h in range(2):
                part = pl.ds(h * PANEL, PANEL)
                ref[pl.ds(r, n), part] = mm(order_ref[pl.ds(r, n)], front[:, part]).astype(BF16)

    ordered(fs, s0, leaf, CHUNKS)
    copies[1].wait()
    for r, n in CHUNKS:
        fac[pl.ds(r, n)] = factor_of(fs[pl.ds(r, n), pl.ds(0, PANEL)], dinv0)
    copies[0].wait()
    y_landed(0)
    got = d1.at[pl.ds(pl.multiple_of((1 - bit0) * 256 + c * 128, 128), 128)]
    arrived(got, recv_sem.at[0])
    send(got, got, 18, inner(0, 0, 1))

    q = iota((1, PANEL), 1)
    block = (q >> 4) & 7
    dist = jnp.where(block & 1 == 1, (block + 1) >> 1, -(block >> 1))
    x_from = xh ^ ((q >> 7) & 1)
    y_from = (y + dist + 8) & 7
    j_from = x_from * 16 + y_from * 2 + (c ^ (q >> 8))
    i = q & 15
    targets = (
        (bit0 ^ (i >> 3)) * 256 + j_from * 8 + (i & 7),
        ((bit0 + 2 * bit1) ^ (i >> 2)) * 128 + j_from * 4 + (i & 3),
    )
    down = iota((PANEL, PANEL), 0)
    for lvl in range(2):
        perm[lvl] = hot(targets[lvl] == down)

    def one_of(ref, *columns):
        i = iota(ref.shape, 0)
        k = iota(ref.shape, 1)
        hit = k == columns[0](i)
        for column in columns[1:]:
            hit = hit | (k == column(i))
        ref[...] = hot(hit)

    one_of(
        pick1, lambda i: i, lambda i: jnp.where(i < 8, i + 24, i + 8), lambda i: jnp.where(i < 8, i + 32, i + 40)
    )
    one_of(
        pick2,
        lambda i: (i >> 2) * 16 + (i & 3), lambda i: ((i >> 2) ^ 2) * 16 + 4 + (i & 3), lambda i: 64 + (i >> 2) * 16 + (i & 3),
    )
    copies[6].wait()
    pm[pl.ds(32, TILE)] = mid[pl.ds(0, TILE), pl.ds(0, PANEL)]
    ordering(s1, e1, rank1, 4, 1)
    x_landed(0)
    gather_end(0)

    def landing(ref, mine, far, sem, live_rows):
        arrived(codes.at[far], recv_sem.at[sem])
        at = jnp.where(lanes < HALF, codes[mine, 0:1, :], codes[far, 0:1, :] - ROWS)
        for r in range(0, ROWS, 160):
            row = iota((160, ROWS), 0) + r
            hit = row.astype(F32) == at
            if live_rows is not None:
                hit = hit & (row < live_rows)
            ref[pl.ds(r, 160)] = hot(hit)

    def update(front, factor, rows):
        product = mmt(factor[rows], piv[...])
        return (front[rows, pl.ds(PANEL, PANEL)].astype(F32) - product).astype(BF16)

    def far_updates(front, factor, store, other, sem, flip):
        later = []
        for k, (r, n) in enumerate(FAR_CHUNKS):
            at = r - FAR_CHUNKS[0][0]
            store[pl.ds(at, n)] = update(front, factor, pl.ds(r, n))
            later.append((store.at[pl.ds(at, n)], other.at[pl.ds(HALF + at, n)], sem + k, subs(flip)))
        return later

    def own_updates(front, factor, other):
        for r, n in OWN_CHUNKS:
            other[pl.ds(r - TILE, n)] = update(front, factor, pl.ds(r, n))

    def first_part(front, place, other, chunks):
        for r, n in chunks:
            rows = pl.ds(r, n)
            acc[rows] = front[rows, pl.ds(0, PANEL)].astype(F32) + mm(place[rows, pl.ds(0, 256)], other[pl.ds(0, 256)])

    def second_part(place, other, sem, chunks):
        arrived(other.at[pl.ds(HALF, 192)], recv_sem.at[sem])
        for r, n in chunks:
            rows = pl.ds(r, n)
            acc[rows] += mm(place[rows, pl.ds(256, 256)], other[pl.ds(256, 256)])

    def last_part(place, other, sem, chunks, inv, factor, live_rows):
        arrived(other.at[pl.ds(512, 128)], recv_sem.at[sem])
        for r, n in chunks:
            rows = pl.ds(r, n)
            whole = acc[rows] + mm(place[rows, pl.ds(512, 128)], other[pl.ds(512, 128)])
            if live_rows is not None:
                whole = jnp.where((iota((n, PANEL), 0) + r) < live_rows, whole, 0.0)
            factor[rows] = factor_of(whole.astype(BF16), inv)

    pm[pl.ds(0, TILE)] = update(fs, fac, pl.ds(0, TILE))
    send(pm.at[pl.ds(0, TILE)], pm.at[pl.ds(16, TILE)], 10, subs(1))
    later = far_updates(fs, fac, y0, x0, 11, 1)
    copies[8].wait()
    arrived(d1.at[pl.ds(pl.multiple_of((1 - bit0) * 256 + (1 - c) * 128, 128), 128)], recv_sem.at[18])
    arrived(pm.at[pl.ds(48, TILE)], recv_sem.at[4])
    arrived(pm.at[pl.ds(16, TILE)], recv_sem.at[10])
    g[0, pl.ds(0, TILE)] = factor_of(mm(pick1[...], pm[...]).astype(BF16), d1)
    gather_start(1, g.at[0, pl.ds(0, TILE)])
    for part in later:
        send(*part)
    own_updates(fs, fac, x0)
    quarters = (0, 1 - bit0 + 2 * bit1, bit0 + 2 - 2 * bit1, 3 - bit0 - 2 * bit1)
    for f in (1, 2, 3):
        got = d2.at[pl.ds(pl.multiple_of(quarters[f] * 128 + c * 64, 64), 64)]
        arrived(got, recv_sem.at[f])
        send(got, got, 18 + f, inner(0, 0, 1))
    landing(f0, 0, 1, 8, None)
    for r, n in CHUNKS:
        t1[pl.ds(r, n)] = mm(s1[pl.ds(r, n)], f0[...]).astype(BF16)
    ordered(ms, s1, mid, CHUNKS)
    first_part(ms, t1, x0, CHUNKS)
    y_landed(1)
    copies[7].wait()
    pt[pl.ds(64, TILE)] = top[pl.ds(0, TILE), pl.ds(0, PANEL)]
    second_part(t1, x0, 11, CHUNKS)
    x_landed(1)
    last_part(t1, x0, 12, CHUNKS, d1, fac1, None)
    gather_end(1)

    pt[pl.ds(0, TILE)] = update(ms, fac1, pl.ds(0, TILE))
    for f in (2, 1, 3):
        send(pt.at[pl.ds(0, TILE)], pt.at[pl.ds(16 * f, TILE)], 12 + f, subs(f))
    later = far_updates(ms, fac1, y1, x1, 16, 2)
    copies[9].wait()
    for f in (1, 2, 3):
        arrived(d2.at[pl.ds(pl.multiple_of(quarters[f] * 128 + (1 - c) * 64, 64), 64)], recv_sem.at[18 + f])
        arrived(pt.at[pl.ds(64 + 16 * f, TILE)], recv_sem.at[4 + f])
        arrived(pt.at[pl.ds(16 * f, TILE)], recv_sem.at[12 + f])
    for part in later:
        send(*part)
    g[1, pl.ds(0, TILE)] = factor_of(mm(pick2[...], pt[...]).astype(BF16), d2)
    gather_start(2, g.at[1, pl.ds(0, TILE)])
    even = ((0, 320), (320, 320))
    own_updates(ms, fac1, x1)
    landing(f1, 2, 3, 9, live_f[:, 2:3])
    first_part(top, f1, x1, even)
    y_landed(2)
    x_landed(2)
    second_part(f1, x1, 16, even)
    gather_end(2)
    last_part(f1, x1, 17, even, d2, fac2, live_f[:, 2:3])

    results = []
    for r, n in even:
        rows = pl.ds(r, n)
        alive = (iota((n, PANEL), 0) + r) < live_f[:, 2:3]
        product = mmt(fac2[rows], piv[...])
        res[rows] = jnp.where(alive, top[rows, pl.ds(PANEL, PANEL)].astype(F32) - product, 0.0).astype(BF16)
        results.append(pltpu.make_async_copy(res.at[rows], out.at[rows], local_sem.at[len(results)]))
        results[-1].start()
    for copy in sends:
        copy.wait_send()
    for lvl in range(3):
        ref = fs.at[pl.ds(0, 496), pl.ds(0, PANEL)]
        pltpu.make_async_remote_copy(
            src_ref=ref, dst_ref=ref, send_sem=g_send.at[lvl], recv_sem=g_recv.at[lvl, 0],
            device_id=subs(1), device_id_type=MESH,
        ).wait_send()
    for copy in results:
        copy.wait()


def per_device(leaf, mid, top, dinv0, dinv1, dinv2, live_rows, map0, map1):
    hbm = pl.BlockSpec(memory_space=pl.ANY)
    held = lambda *shape: pltpu.VMEM(shape, BF16)
    more = ROWS + TILE
    return pl.pallas_call(
        body,
        name="panel_steps",
        out_shape=jax.ShapeDtypeStruct((ROWS, PANEL), BF16),
        in_specs=[hbm] * 9,
        out_specs=hbm,
        scratch_shapes=[
            held(2, 8, 2, TILE, PANEL),
            held(ROWS, 1024),
            held(ROWS, 1024),
            held(ROWS, 1024),
            held(PANEL, BLOCK),
            pltpu.VMEM((1, 3), jnp.int32),
            pltpu.VMEM((ROWS,), jnp.int32),
            pltpu.VMEM((ROWS,), jnp.int32),
            held(PANEL, BLOCK),
            held(PANEL, BLOCK),
            held(more, ROWS),
            held(more, ROWS),
            held(ROWS, ROWS),
            held(ROWS, ROWS),
            held(more, ROWS),
            held(more, 1024),
            held(more, 1024),
            held(more, PANEL),
            held(more, PANEL),
            held(ROWS, PANEL),
            held(2, PANEL, PANEL),
            held(PANEL, PANEL),
            held(2, PANEL, PANEL),
            held(ROWS, PANEL),
            held(ROWS, PANEL),
            held(HALF, PANEL),
            held(HALF, PANEL),
            held(64, PANEL),
            held(128, PANEL),
            held(TILE, 64),
            held(TILE, 128),
            pltpu.VMEM((more, PANEL), F32),
            held(ROWS, PANEL),
            pltpu.VMEM((4, 8, ROWS), F32),
            pltpu.SemaphoreType.DMA((10,)),
            pltpu.SemaphoreType.DMA((24,)),
            pltpu.SemaphoreType.DMA((22,)),
            pltpu.SemaphoreType.DMA((3,)),
            pltpu.SemaphoreType.DMA((3, 7)),
        ],
        compiler_params=pltpu.CompilerParams(
            collective_id=0, has_side_effects=True, vmem_limit_bytes=60 * 2**20
        ),
    )(leaf, mid, top, dinv0, dinv1, dinv2, live_rows.reshape(1, 3), map0, map1)


def solution(mesh):
    rows = P(("sub", "inner"), None)
    placed = (
        rows, rows, rows, P("sub", None), P("sub", None), P("sub", None),
        P(None, ("sub", "inner")), P(("sub", "inner")), P(("sub", "inner")),
    )
    return jax.shard_map(per_device, mesh=mesh, in_specs=placed, out_specs=rows, check_vma=False)
```

```python
import jax
import jax.numpy as jnp
from jax import lax
from jax.experimental import pallas as pl
from jax.experimental.pallas import tpu as pltpu
from jax.sharding import PartitionSpec as P

ROWS = 640
PANEL = 512
BLOCK = 256
HALF = ROWS // 2
TILE = 16
INNER = 32
F32 = jnp.float32
BF16 = jnp.bfloat16
MESH = pl.DeviceIdType.MESH

AWAY = (0, 1, -1, 2, -2, 3, -3, 4)
FAR_FIRST = (4, 3, -3, 2, -2, 1, -1)
SLOT = {d: i for i, d in enumerate(AWAY)}
BACK = {d: SLOT[-d] if -d in SLOT else SLOT[d] for d in AWAY}
CHUNKS = ((0, 336), (336, 320))
OWN_CHUNKS = ((16, 320),)
FAR_CHUNKS = ((336, 192), (528, 128))


def mm(a, b):
    return lax.dot_general(a, b, (((1,), (0,)), ((), ())), preferred_element_type=F32)


def mmt(a, b):
    return lax.dot_general(a, b, (((1,), (1,)), ((), ())), preferred_element_type=F32)


def iota(shape, dim):
    return lax.broadcasted_iota(jnp.int32, shape, dim)


def hot(cond):
    return jnp.where(cond, 1.0, 0.0).astype(BF16)


def factor_of(panel, inv):
    return jnp.concatenate(
        [mmt(panel[:, b * BLOCK : (b + 1) * BLOCK], inv[b * BLOCK : (b + 1) * BLOCK, :]) for b in range(2)], 1
    ).astype(BF16)


def columns_of(row):
    return jnp.broadcast_to(row, (128, ROWS)).T


def body(
    leaf_hbm, mid_hbm, top_hbm, dinv0_hbm, dinv1_hbm, dinv2_hbm, live_hbm, map0_hbm, map1_hbm, out,
    lead, leaf, mid, top, dinv0, live, map0, map1, d1, d2, s0, s1, f0, f1, t1, fs, ms, fac, fac1, fac2,
    g, piv, perm, x0, x1, y0, y1, pm, pt, pick1, pick2, acc, res, codes, local_sem, send_sem, recv_sem, g_send, g_recv,
):
    s = lax.axis_index("sub")
    j = lax.axis_index("inner")
    bit0 = lax.rem(s, 2)
    bit1 = lax.rem(lax.div(s, 2), 2)
    xh = lax.div(j, 16)
    y = lax.rem(lax.div(j, 2), 8)
    c = lax.rem(j, 2)
    near1 = s + 1 - 2 * bit0
    near2 = s + 2 - 4 * bit1
    near3 = near1 + 2 - 4 * bit1

    def inner(flip_x, dist, flip_c):
        xs = 1 - xh if flip_x else xh
        cs = 1 - c if flip_c else c
        return (s, xs * 16 + lax.rem(y + dist + 8, 8) * 2 + cs)

    def subs(flip):
        return ((s, near1, near2, near3)[flip], j)

    copies = [
        pltpu.make_async_copy(leaf_hbm.at[pl.ds(0, TILE), pl.ds(0, PANEL)], lead.at[xh, y, c], local_sem.at[0]),
        pltpu.make_async_copy(dinv0_hbm, dinv0, local_sem.at[1]),
        pltpu.make_async_copy(map0_hbm, map0, local_sem.at[2]),
        pltpu.make_async_copy(map1_hbm, map1, local_sem.at[3]),
        pltpu.make_async_copy(live_hbm, live, local_sem.at[4]),
        pltpu.make_async_copy(leaf_hbm, leaf, local_sem.at[5]),
        pltpu.make_async_copy(mid_hbm, mid, local_sem.at[6]),
        pltpu.make_async_copy(top_hbm, top, local_sem.at[7]),
        pltpu.make_async_copy(dinv1_hbm, d1.at[pl.ds(pl.multiple_of(bit0 * 256, 256), 256)], local_sem.at[8]),
        pltpu.make_async_copy(
            dinv2_hbm, d2.at[pl.ds(pl.multiple_of((bit0 + 2 * bit1) * 128, 128), 128)], local_sem.at[9]
        ),
    ]
    barrier = pltpu.get_barrier_semaphore()
    partners = [inner(0, d, 0) for d in FAR_FIRST] + [inner(1, d, 0) for d in AWAY[:5]] + [inner(1, 0, 1), inner(0, 0, 1)]
    partners += [subs(f) for f in (1, 2, 3)]
    for partner in partners:
        pl.semaphore_signal(barrier, inc=1, device_id=partner, device_id_type=MESH)

    for copy in copies:
        copy.start()
    pl.semaphore_wait(barrier, len(partners))

    sends = []

    def send(src, dst, sem, target):
        copy = pltpu.make_async_remote_copy(
            src_ref=src, dst_ref=dst, send_sem=send_sem.at[len(sends)], recv_sem=recv_sem.at[sem],
            device_id=target, device_id_type=MESH,
        )
        copy.start()
        sends.append(copy)

    def arrived(ref, sem):
        pltpu.make_async_remote_copy(
            src_ref=ref, dst_ref=ref, send_sem=send_sem.at[0], recv_sem=sem, device_id=subs(1), device_id_type=MESH
        ).wait_recv()

    def g_copy(lvl, src, dst, sem, target):
        pltpu.make_async_remote_copy(
            src_ref=src, dst_ref=dst, send_sem=g_send.at[lvl], recv_sem=g_recv.at[lvl, sem],
            device_id=target, device_id_type=MESH,
        ).start()

    def place(lvl, flip_x, d, mine):
        if lvl == 0:
            return lead.at[xh, y, c] if mine else lead.at[1 - xh if flip_x else xh, lax.rem(y + d + 8, 8), c]
        return g.at[lvl - 1, pl.ds(128 * flip_x + (BACK[d] if mine else SLOT[d]) * TILE, TILE)]

    def column(lvl, flip_x, flip_c):
        if lvl == 0:
            return lead.at[1 - xh if flip_x else xh, :, 1 - c if flip_c else c]
        return g.at[lvl - 1, pl.ds(256 * flip_c + 128 * flip_x, 128)]

    def four(lvl):
        return lead.at[0, pl.ds(0, 4), 0] if lvl == 0 else g.at[lvl - 1, pl.ds(16, 64)]

    def gather_start(lvl, own):
        for d in FAR_FIRST:
            g_copy(lvl, own, place(lvl, 0, d, True), 6 if abs(d) > 2 else 0, inner(0, d, 0))
        for d in FAR_FIRST[3:] + (0,):
            g_copy(lvl, own, place(lvl, 1, d, True), 1, inner(1, d, 0))

    def y_landed(lvl):
        arrived(three(lvl, 0), g_recv.at[lvl, 6])
        for d in FAR_FIRST[:3]:
            part = place(lvl, 0, d, False)
            for flip_c in (0, 1):
                to = part if lvl == 0 else g.at[lvl - 1, pl.ds(256 * flip_c + 128 + SLOT[d] * TILE, TILE)]
                g_copy(lvl, part, to, 4 + flip_c, inner(1, 0, flip_c))
        arrived(four(lvl), g_recv.at[lvl, 0])
        part = column(lvl, 0, 0)
        g_copy(lvl, part, part if lvl == 0 else column(lvl, 0, 1), 2, inner(0, 0, 1))

    def five(lvl):
        return lead.at[0, pl.ds(0, 5), 0] if lvl == 0 else g.at[lvl - 1, pl.ds(128, 80)]

    def three(lvl, flip_c):
        return lead.at[0, pl.ds(0, 3), 0] if lvl == 0 else g.at[lvl - 1, pl.ds(256 * flip_c + 208, 48)]

    def x_landed(lvl):
        arrived(five(lvl), g_recv.at[lvl, 1])
        if lvl == 0:
            for d in (0,) + FAR_FIRST[3:]:
                part = place(0, 1, d, False)
                g_copy(lvl, part, part, 3, inner(0, 0, 1))
        else:
            g_copy(lvl, five(lvl), g.at[lvl - 1, pl.ds(384, 80)], 3, inner(0, 0, 1))

    def gather_end(lvl):
        arrived(three(lvl, 0), g_recv.at[lvl, 4])
        if lvl > 0:
            half = mm(perm[lvl - 1, :, pl.ds(0, 256)], g[lvl - 1, pl.ds(0, 256)])
        arrived(column(lvl, 0, 1), g_recv.at[lvl, 2])
        arrived(five(lvl) if lvl == 0 else g.at[lvl - 1, pl.ds(384, 80)], g_recv.at[lvl, 3])
        arrived(three(lvl, 1), g_recv.at[lvl, 5])
        if lvl > 0:
            half += mm(perm[lvl - 1, :, pl.ds(256, 256)], g[lvl - 1, pl.ds(256, 256)])
            piv[...] = half.astype(BF16)
        else:
            piv[...] = factor_of(lead[...].reshape(PANEL, PANEL), dinv0)

    gather_start(0, leaf_hbm.at[pl.ds(0, TILE), pl.ds(0, PANEL)])
    quarter = pl.ds(pl.multiple_of((bit0 + 2 * bit1) * 128 + c * 64, 64), 64)
    half = pl.ds(pl.multiple_of(bit0 * 256 + c * 128, 128), 128)
    send(dinv1_hbm.at[pl.ds(pl.multiple_of(c * 128, 128), 128)], d1.at[half], 0, subs(1))
    send(mid_hbm.at[pl.ds(0, TILE), pl.ds(0, PANEL)], pm.at[pl.ds(48, TILE)], 4, subs(1))
    for f in (1, 2, 3):
        send(top_hbm.at[pl.ds(0, TILE), pl.ds(0, PANEL)], pt.at[pl.ds(64 + 16 * f, TILE)], 4 + f, subs(f))
        send(dinv2_hbm.at[pl.ds(pl.multiple_of(c * 64, 64), 64)], d2.at[quarter], f, subs(f))

    def order(codes_row):
        down = columns_of(codes_row)[:, 0:1]
        rank = jnp.sum(jnp.where(down < codes_row, 1.0, 0.0), axis=0, keepdims=True)
        rank_down = columns_of(rank)[:, 0:1]
        at = iota((ROWS, ROWS), 1).astype(F32)
        return rank, jnp.sum(jnp.where(rank_down == at, down, 0.0), axis=0, keepdims=True)

    for copy in copies[2:5]:
        copy.wait()
    e0 = map0[...].astype(F32).reshape(1, ROWS)
    e1 = map1[...].astype(F32).reshape(1, ROWS)
    rank0, sorted0 = order(e0)
    codes[0] = jnp.broadcast_to(sorted0, (8, ROWS))
    send(codes.at[0], codes.at[1], 8, subs(1))
    rank1, sorted1 = order(e1)
    codes[2] = jnp.broadcast_to(sorted1, (8, ROWS))
    send(codes.at[2], codes.at[3], 9, subs(2))

    lanes = iota((1, ROWS), 1)
    live_f = live[...]

    def ordering(ref, codes_row, rank, early, level):
        alive = lanes < live_f[:, level : level + 1]
        slot = iota((TILE, ROWS), 0)
        wanted = jnp.where(slot < early, slot, jnp.where(slot < 2 * early, ROWS - early + slot, -1)).astype(F32)
        ref[pl.ds(0, TILE)] = hot((codes_row == wanted) & alive)
        for r, n in ((16, 160), (176, 160), (336, 160), (496, 160)):
            ref[pl.ds(r, n)] = hot((rank == (iota((n, ROWS), 0) + (r - TILE)).astype(F32)) & alive)

    ordering(s0, e0, rank0, 8, 0)
    copies[5].wait()

    def ordered(ref, order_ref, front, chunks):
        for r, n in chunks:
            for h in range(2):
                part = pl.ds(h * PANEL, PANEL)
                ref[pl.ds(r, n), part] = mm(order_ref[pl.ds(r, n)], front[:, part]).astype(BF16)

    ordered(fs, s0, leaf, CHUNKS)
    copies[1].wait()
    for r, n in CHUNKS:
        fac[pl.ds(r, n)] = factor_of(fs[pl.ds(r, n), pl.ds(0, PANEL)], dinv0)
    copies[0].wait()
    y_landed(0)
    got = d1.at[pl.ds(pl.multiple_of((1 - bit0) * 256 + c * 128, 128), 128)]
    arrived(got, recv_sem.at[0])
    send(got, got, 18, inner(0, 0, 1))

    q = iota((1, PANEL), 1)
    block = (q >> 4) & 7
    dist = jnp.where(block & 1 == 1, (block + 1) >> 1, -(block >> 1))
    x_from = xh ^ ((q >> 7) & 1)
    y_from = (y + dist + 8) & 7
    j_from = x_from * 16 + y_from * 2 + (c ^ (q >> 8))
    i = q & 15
    targets = (
        (bit0 ^ (i >> 3)) * 256 + j_from * 8 + (i & 7),
        ((bit0 + 2 * bit1) ^ (i >> 2)) * 128 + j_from * 4 + (i & 3),
    )
    down = iota((PANEL, PANEL), 0)
    for lvl in range(2):
        perm[lvl] = hot(targets[lvl] == down)

    def one_of(ref, *columns):
        i = iota(ref.shape, 0)
        k = iota(ref.shape, 1)
        hit = k == columns[0](i)
        for column in columns[1:]:
            hit = hit | (k == column(i))
        ref[...] = hot(hit)

    one_of(
        pick1, lambda i: i, lambda i: jnp.where(i < 8, i + 24, i + 8), lambda i: jnp.where(i < 8, i + 32, i + 40)
    )
    one_of(
        pick2,
        lambda i: (i >> 2) * 16 + (i & 3), lambda i: ((i >> 2) ^ 2) * 16 + 4 + (i & 3), lambda i: 64 + (i >> 2) * 16 + (i & 3),
    )
    copies[6].wait()
    pm[pl.ds(32, TILE)] = mid[pl.ds(0, TILE), pl.ds(0, PANEL)]
    ordering(s1, e1, rank1, 4, 1)
    x_landed(0)
    gather_end(0)

    def landing(ref, mine, far, sem, live_rows):
        arrived(codes.at[far], recv_sem.at[sem])
        at = jnp.where(lanes < HALF, codes[mine, 0:1, :], codes[far, 0:1, :] - ROWS)
        for r in range(0, ROWS, 160):
            row = iota((160, ROWS), 0) + r
            hit = row.astype(F32) == at
            if live_rows is not None:
                hit = hit & (row < live_rows)
            ref[pl.ds(r, 160)] = hot(hit)

    def update(front, factor, rows):
        product = mmt(factor[rows], piv[...])
        return (front[rows, pl.ds(PANEL, PANEL)].astype(F32) - product).astype(BF16)

    def far_updates(front, factor, store, other, sem, flip):
        later = []
        for k, (r, n) in enumerate(FAR_CHUNKS):
            at = r - FAR_CHUNKS[0][0]
            store[pl.ds(at, n)] = update(front, factor, pl.ds(r, n))
            later.append((store.at[pl.ds(at, n)], other.at[pl.ds(HALF + at, n)], sem + k, subs(flip)))
        return later

    def own_updates(front, factor, other):
        for r, n in OWN_CHUNKS:
            other[pl.ds(r - TILE, n)] = update(front, factor, pl.ds(r, n))

    def first_part(front, place, other, chunks):
        for r, n in chunks:
            rows = pl.ds(r, n)
            acc[rows] = front[rows, pl.ds(0, PANEL)].astype(F32) + mm(place[rows, pl.ds(0, 256)], other[pl.ds(0, 256)])

    def second_part(place, other, sem, chunks):
        arrived(other.at[pl.ds(HALF, 192)], recv_sem.at[sem])
        for r, n in chunks:
            rows = pl.ds(r, n)
            acc[rows] += mm(place[rows, pl.ds(256, 256)], other[pl.ds(256, 256)])

    def last_part(place, other, sem, chunks, inv, factor, live_rows, then=None):
        arrived(other.at[pl.ds(512, 128)], recv_sem.at[sem])
        for r, n in chunks:
            rows = pl.ds(r, n)
            whole = acc[rows] + mm(place[rows, pl.ds(512, 128)], other[pl.ds(512, 128)])
            if live_rows is not None:
                whole = jnp.where((iota((n, PANEL), 0) + r) < live_rows, whole, 0.0)
            factor[rows] = factor_of(whole.astype(BF16), inv)
            if then is not None:
                then(r, n)

    pm[pl.ds(0, TILE)] = update(fs, fac, pl.ds(0, TILE))
    send(pm.at[pl.ds(0, TILE)], pm.at[pl.ds(16, TILE)], 10, subs(1))
    later = far_updates(fs, fac, y0, x0, 11, 1)
    copies[8].wait()
    arrived(d1.at[pl.ds(pl.multiple_of((1 - bit0) * 256 + (1 - c) * 128, 128), 128)], recv_sem.at[18])
    arrived(pm.at[pl.ds(48, TILE)], recv_sem.at[4])
    arrived(pm.at[pl.ds(16, TILE)], recv_sem.at[10])
    g[0, pl.ds(0, TILE)] = factor_of(mm(pick1[...], pm[...]).astype(BF16), d1)
    gather_start(1, g.at[0, pl.ds(0, TILE)])
    for part in later:
        send(*part)
    own_updates(fs, fac, x0)
    quarters = (0, 1 - bit0 + 2 * bit1, bit0 + 2 - 2 * bit1, 3 - bit0 - 2 * bit1)
    for f in (1, 2, 3):
        got = d2.at[pl.ds(pl.multiple_of(quarters[f] * 128 + c * 64, 64), 64)]
        arrived(got, recv_sem.at[f])
        send(got, got, 18 + f, inner(0, 0, 1))
    landing(f0, 0, 1, 8, None)
    for r, n in CHUNKS:
        t1[pl.ds(r, n)] = mm(s1[pl.ds(r, n)], f0[...]).astype(BF16)
    ordered(ms, s1, mid, CHUNKS)
    first_part(ms, t1, x0, CHUNKS)
    y_landed(1)
    copies[7].wait()
    pt[pl.ds(64, TILE)] = top[pl.ds(0, TILE), pl.ds(0, PANEL)]
    second_part(t1, x0, 11, CHUNKS)
    x_landed(1)
    last_part(t1, x0, 12, CHUNKS, d1, fac1, None)
    gather_end(1)

    pt[pl.ds(0, TILE)] = update(ms, fac1, pl.ds(0, TILE))
    for f in (3, 2, 1):
        send(pt.at[pl.ds(0, TILE)], pt.at[pl.ds(16 * f, TILE)], 12 + f, subs(f))
    later = far_updates(ms, fac1, y1, x1, 16, 2)
    copies[9].wait()
    for f in (1, 2, 3):
        arrived(d2.at[pl.ds(pl.multiple_of(quarters[f] * 128 + (1 - c) * 64, 64), 64)], recv_sem.at[18 + f])
        arrived(pt.at[pl.ds(64 + 16 * f, TILE)], recv_sem.at[4 + f])
        arrived(pt.at[pl.ds(16 * f, TILE)], recv_sem.at[12 + f])
    for part in later:
        send(*part)
    g[1, pl.ds(0, TILE)] = factor_of(mm(pick2[...], pt[...]).astype(BF16), d2)
    gather_start(2, g.at[1, pl.ds(0, TILE)])
    even = ((0, 320), (320, 320))
    own_updates(ms, fac1, x1)
    landing(f1, 2, 3, 9, live_f[:, 2:3])
    first_part(top, f1, x1, even)
    y_landed(2)
    x_landed(2)
    second_part(f1, x1, 16, even)
    gather_end(2)
    results = []

    def finish(r, n):
        rows = pl.ds(r, n)
        alive = (iota((n, PANEL), 0) + r) < live_f[:, 2:3]
        product = mmt(fac2[rows], piv[...])
        res[rows] = jnp.where(alive, top[rows, pl.ds(PANEL, PANEL)].astype(F32) - product, 0.0).astype(BF16)
        results.append(pltpu.make_async_copy(res.at[rows], out.at[rows], local_sem.at[len(results)]))
        results[-1].start()

    last_part(f1, x1, 17, even, d2, fac2, live_f[:, 2:3], finish)

    for copy in sends:
        copy.wait_send()
    for lvl in range(3):
        ref = fs.at[pl.ds(0, 496), pl.ds(0, PANEL)]
        pltpu.make_async_remote_copy(
            src_ref=ref, dst_ref=ref, send_sem=g_send.at[lvl], recv_sem=g_recv.at[lvl, 0],
            device_id=subs(1), device_id_type=MESH,
        ).wait_send()
    for copy in results:
        copy.wait()


def per_device(leaf, mid, top, dinv0, dinv1, dinv2, live_rows, map0, map1):
    hbm = pl.BlockSpec(memory_space=pl.ANY)
    held = lambda *shape: pltpu.VMEM(shape, BF16)
    more = ROWS + TILE
    return pl.pallas_call(
        body,
        name="panel_steps",
        out_shape=jax.ShapeDtypeStruct((ROWS, PANEL), BF16),
        in_specs=[hbm] * 9,
        out_specs=hbm,
        scratch_shapes=[
            held(2, 8, 2, TILE, PANEL),
            held(ROWS, 1024),
            held(ROWS, 1024),
            held(ROWS, 1024),
            held(PANEL, BLOCK),
            pltpu.VMEM((1, 3), jnp.int32),
            pltpu.VMEM((ROWS,), jnp.int32),
            pltpu.VMEM((ROWS,), jnp.int32),
            held(PANEL, BLOCK),
            held(PANEL, BLOCK),
            held(more, ROWS),
            held(more, ROWS),
            held(ROWS, ROWS),
            held(ROWS, ROWS),
            held(more, ROWS),
            held(more, 1024),
            held(more, 1024),
            held(more, PANEL),
            held(more, PANEL),
            held(ROWS, PANEL),
            held(2, PANEL, PANEL),
            held(PANEL, PANEL),
            held(2, PANEL, PANEL),
            held(ROWS, PANEL),
            held(ROWS, PANEL),
            held(HALF, PANEL),
            held(HALF, PANEL),
            held(64, PANEL),
            held(128, PANEL),
            held(TILE, 64),
            held(TILE, 128),
            pltpu.VMEM((more, PANEL), F32),
            held(ROWS, PANEL),
            pltpu.VMEM((4, 8, ROWS), F32),
            pltpu.SemaphoreType.DMA((10,)),
            pltpu.SemaphoreType.DMA((24,)),
            pltpu.SemaphoreType.DMA((22,)),
            pltpu.SemaphoreType.DMA((3,)),
            pltpu.SemaphoreType.DMA((3, 7)),
        ],
        compiler_params=pltpu.CompilerParams(
            collective_id=0, has_side_effects=True, vmem_limit_bytes=60 * 2**20
        ),
    )(leaf, mid, top, dinv0, dinv1, dinv2, live_rows.reshape(1, 3), map0, map1)


def solution(mesh):
    rows = P(("sub", "inner"), None)
    placed = (
        rows, rows, rows, P("sub", None), P("sub", None), P("sub", None),
        P(None, ("sub", "inner")), P(("sub", "inner")), P(("sub", "inner")),
    )
    return jax.shard_map(per_device, mesh=mesh, in_specs=placed, out_specs=rows, check_vma=False)
```
